256 devices in a mesh: tensor: 8 (over y, core), expert: 8 (over x, z_hi), dp: 4 (over z_lo).
Axes of the slice: x: 4, y: 4, z: 8 (z_hi: 2, z_lo: 4; z = z_hi * 4 + z_lo), core: 2. Of those that a mesh axis runs over, the one named last changes fastest.
Arguments:
- tokens: bfloat16 [4096, 3072], P(('expert', 'dp'), 'tensor'), may hold values from -6 to 6
- routes: int32 [4096, 2], P(('expert', 'dp')), may hold values from 0 to 7, all different within a row; in each aligned block of 128 rows (0 to 127, 128 to 255, ...) at most 64 rows name the same one
- up_weight: bfloat16 [8, 3072, 16384], P('expert', 'dp', 'tensor'), may hold values from -0.109375 to 0.109375
- saved_pre: bfloat16 [8, 2048, 16384], P('expert', 'dp', 'tensor'), may hold values from -6 to 6
- grad_act: bfloat16 [8, 2048, 16384], P('expert', 'dp', 'tensor'), may hold values from -1.5 to 1.5
Outputs:
- token_grad: bfloat16 [4096, 3072], P(('expert', 'dp'), 'tensor')
- up_grad: bfloat16 [8, 3072, 16384], P('expert', 'dp', 'tensor')
The draws below stay inside these ranges and needn't reach their ends.
Inputs may be any that keep to these rules, and one draw needn't show every extreme that they name: `routes`: the two experts of a token differ. Among the 128 tokens of one source group no expert is named by more than 64 tokens.
All inputs are finite; a program needn't handle non-finite values.
Results may differ from the reference program's by a relative error of at most 0.02.
Values may be sent and summed in bfloat16 or wider, within the bound.
No kernel may reach another device: no remote copies, remote signals or barrier semaphores. Data moves between devices by JAX's collectives and lax.ppermute only.
A program may use at most 128 MiB of HBM per device.

```python
import math
from functools import partial
import jax
import jax.numpy as jnp
import numpy as np
from jax import lax

D = 3072
FF = 16384
TOK_DEV = 128
EXPERTS = 8
CAP = 64
SLOTS = 512
TOKENS = 4096
N_EXPERT = 8
N_DP = 4


def block_scale(own_key, dims, pieces, least, largest):
    def one(dim, blocks):
        draws = jax.random.uniform(jax.random.fold_in(jax.random.fold_in(own_key, 6), dim), (blocks,), jnp.float32, least / len(pieces), largest / len(pieces))
        return jnp.repeat(jnp.exp(draws), dims[dim] // blocks).reshape((-1,) + (1,) * (len(dims) - dim - 1))

    factor_of = one(*pieces[0])
    for cut in pieces[1:]:
        factor_of = factor_of * one(*cut)
    return factor_of


def deal_out(key, own, number, rows, amount, top, most, lean):
    ranking = jax.random.permutation(key, amount)
    crowded, common = portions_of(amount, rows * top, most, lean, True), portions_of(amount, rows * top, most, lean, False)
    places = jnp.arange(amount)

    def named(lengths, turn):
        used = int((lengths > 0).sum())
        fixed = max(1, used // 4)
        shifted = fixed + (places - fixed + turn * (used - fixed)) % max(1, amount - fixed)
        return jnp.zeros((amount,), jnp.int32).at[ranking[jnp.where(places < fixed, places, shifted)]].set(jnp.asarray(lengths, jnp.int32))

    lengths = jnp.where(number % 4 == 0, named(crowded, number // 4), named(common, number - number // 4 - 1))
    mixed = jax.random.permutation(jax.random.fold_in(own, 3), amount)
    giver, sink = mixed[0:amount // 2 * 2:2], mixed[1:amount // 2 * 2:2]
    margin = jnp.minimum(lengths[giver] - 1, most - lengths[sink]) // 2
    margin = jnp.where((giver == ranking[0]) | (sink == ranking[0]) | (lengths[sink] == 0), 0, jnp.maximum(margin, 0))
    shifted = jax.random.randint(jax.random.fold_in(own, 4), (amount // 2,), 0, 1 << 20) % (margin + 1)
    lengths = lengths.at[giver].add(-shifted).at[sink].add(shifted)
    items = jnp.searchsorted(jnp.cumsum(lengths), jnp.arange(rows * top), side="right").astype(jnp.int32)
    listing = items.reshape(top, rows).T
    listing = listing[jax.random.permutation(jax.random.fold_in(own, 1), rows)]
    turn = jax.random.randint(jax.random.fold_in(own, 2), (rows, 1), 0, top)
    return jnp.take_along_axis(listing, (jnp.arange(top)[None, :] + turn) % top, axis=1)


def portions_of(number_of, total, reach, lean, full):
    portions = [(1 << 20) // math.isqrt(standing ** lean) + 1 for standing in range(1, number_of + 1)]
    largest = reach if full else min(reach, max(-(-total // number_of), total * portions[0] // sum(portions)))
    least = 1 if total - largest >= number_of - 1 else 0
    given, surplus = [largest] + [least] * (number_of - 1), total - largest - least * (number_of - 1)
    while surplus > 0:
        movable = [i for i in range(1, number_of) if given[i] < largest] or [i for i in range(1, number_of) if given[i] < reach]
        mass, left = sum([portions[i] for i in movable]), surplus
        for i in movable:
            more = min(reach - given[i], max(1, left * portions[i] // mass), surplus)
            given[i] = given[i] + more
            surplus = surplus - more
    return np.array(given)


def normal_values(key, extent, width, most, shards=(), kind=jnp.bfloat16):
    result = jax.random.normal(key, extent, jnp.float32) * width
    if len(shards) > 0:
        result = block_scale(key, extent, shards, -0.22, 0.18) * result
    return jnp.clip(result, min=-most, max=most).astype(kind)


def setup_inputs(seed: int = 0) -> dict:
    keys = jax.random.split(jax.random.key(seed), 6)
    tokens = normal_values(keys[0], (TOKENS, D), 1.0, 6.0, ((0, 32), (1, 8)))
    routes_keys = jax.random.split(jax.random.fold_in(keys[1], 1), TOKENS // TOK_DEV)
    routes_turns = jax.random.permutation(jax.random.fold_in(keys[1], 3), TOKENS // TOK_DEV)
    routes = jax.vmap(lambda own, number: deal_out(jax.random.fold_in(keys[1], 2), own, number, TOK_DEV, EXPERTS, 2, CAP, 2))(routes_keys, routes_turns).reshape((TOKENS, 2))
    up_weight = normal_values(keys[2], (EXPERTS, D, FF), D ** -0.5, 0.109375, ((0, 8), (1, 4), (2, 8)))
    saved_pre = normal_values(keys[3], (EXPERTS, N_DP * SLOTS, FF), 1.0, 6.0, ((0, 8), (1, 4), (2, 8)))
    grad_act = normal_values(keys[4], (EXPERTS, N_DP * SLOTS, FF), 0.25, 1.5, ((0, 8), (1, 4), (2, 8)))
    return {"tokens": tokens, "routes": routes, "up_weight": up_weight, "saved_pre": saved_pre, "grad_act": grad_act}


root_coef = 0.7978845608028654
cubic_coef = 0.044715


def gelu_slope(pre_act):
    inner_arg = root_coef * (pre_act + cubic_coef * pre_act * pre_act * pre_act)
    tangent = jnp.tanh(inner_arg)
    return 0.5 * (1.0 + tangent) + 0.5 * pre_act * (1.0 - tangent * tangent) * root_coef * (1.0 + 3.0 * cubic_coef * pre_act * pre_act)


def place_slots(route_block, experts, capacity):
    tok_count = route_block.shape[0]
    ordered = jnp.transpose(route_block).reshape(-1)
    onehot = (ordered[:, None] == jnp.arange(experts, dtype=jnp.int32)[None, :]).astype(jnp.int32)
    before = jnp.cumsum(onehot, axis=0) - onehot
    position = jnp.sum(before * onehot, axis=1).astype(jnp.int32)
    return jnp.transpose((ordered * capacity + position).reshape(2, tok_count))


def per_expert(operands):
    rows_in, pre_in, act_in, weight_in = operands
    slot_count = N_EXPERT * CAP
    unit_grad = (act_in.astype(jnp.float32) * gelu_slope(pre_in.astype(jnp.float32))).astype(jnp.bfloat16)
    unit_blocks = unit_grad.reshape(N_DP, slot_count, FF)

    def add_batch(grad_total, batch_pair):
        rows_b, unit_b = batch_pair
        batch_part = lax.dot_general(rows_b, unit_b, (((0,), (0,)), ((), ())), preferred_element_type=jnp.float32).astype(jnp.bfloat16)
        batch_part = lax.optimization_barrier(batch_part)
        return grad_total + batch_part.astype(jnp.float32), None

    grad_total, unused = lax.scan(add_batch, jnp.zeros((D, FF), jnp.float32), (rows_in, unit_blocks))
    slot_grad = lax.dot_general(unit_grad, weight_in, (((1,), (1,)), ((), ())), preferred_element_type=jnp.float32).astype(jnp.bfloat16)
    return grad_total.astype(jnp.bfloat16), slot_grad


def reference(tokens, routes, up_weight, saved_pre, grad_act):
    route_blocks = routes.reshape(N_EXPERT * N_DP, TOK_DEV, 2)
    slot_index = jax.vmap(partial(place_slots, experts=EXPERTS, capacity=CAP))(route_blocks)
    slot_index = slot_index.reshape(N_EXPERT, N_DP, TOK_DEV, 2)
    expert_of = routes.reshape(N_EXPERT, N_DP, TOK_DEV, 2)
    position = slot_index - expert_of * CAP
    source_a = jnp.broadcast_to(jnp.arange(N_EXPERT, dtype=jnp.int32)[:, None, None, None], expert_of.shape)
    source_b = jnp.broadcast_to(jnp.arange(N_DP, dtype=jnp.int32)[None, :, None, None], expert_of.shape)
    values = jnp.broadcast_to(tokens.reshape(N_EXPERT, N_DP, TOK_DEV, 1, D), (N_EXPERT, N_DP, TOK_DEV, 2, D))
    dispatched = jnp.zeros((EXPERTS, N_DP, N_EXPERT, CAP, D), jnp.bfloat16)
    dispatched = dispatched.at[expert_of, source_b, source_a, position].set(values)
    dispatched = dispatched.reshape(EXPERTS, N_DP, N_EXPERT * CAP, D)
    up_grad, slot_grad = lax.map(per_expert, (dispatched, saved_pre, grad_act, up_weight))
    slot_grad = slot_grad.reshape(EXPERTS, N_DP, N_EXPERT, CAP, D)
    picked = slot_grad[expert_of, source_b, source_a, position]
    token_grad = jnp.sum(picked.astype(jnp.float32), axis=3).astype(jnp.bfloat16)
    return token_grad.reshape(TOKENS, D), up_grad
```

```python
import jax
import jax.numpy as jnp
from jax import lax
from jax.sharding import PartitionSpec as P

root_coef = 0.7978845608028654
cubic_coef = 0.044715
n_chunk = 2


def gelu_slope(pre_act):
    inner_arg = root_coef * (pre_act + cubic_coef * pre_act * pre_act * pre_act)
    tangent = jnp.tanh(inner_arg)
    return 0.5 * (1.0 + tangent) + 0.5 * pre_act * (1.0 - tangent * tangent) * root_coef * (
        1.0 + 3.0 * cubic_coef * pre_act * pre_act
    )


def place_slots(route_block, experts, capacity):
    tok_count = route_block.shape[0]
    ordered = jnp.transpose(route_block).reshape(-1)
    onehot = (ordered[:, None] == jnp.arange(experts, dtype=jnp.int32)[None, :]).astype(jnp.int32)
    before = jnp.cumsum(onehot, axis=0) - onehot
    position = jnp.sum(before * onehot, axis=1)
    return (
        jnp.transpose(ordered.reshape(2, tok_count)),
        jnp.transpose(position.reshape(2, tok_count)),
    )


def swap_pairs(back):
    pairs = []
    for b in range(4):
        for d in range(4):
            for core in range(2):
                at_batch = (d * 2 + core) * 4 + b
                at_part = (((d - b) % 4) * 2 + core) * 4 + d
                pairs.append((at_part, at_batch) if back else (at_batch, at_part))
    return pairs


def shift(block, step):
    return lax.ppermute(block, "dp", [(i, i + step) for i in range(4) if 0 <= i + step < 4])


def per_device(tokens, routes, up_weight, saved_pre, grad_act):
    experts = lax.axis_size("expert")
    place = lax.axis_index("dp")
    slot_count, hidden = saved_pre.shape[1:]
    capacity = slot_count // experts
    part = capacity // n_chunk
    tok_dev, width = tokens.shape
    weight = up_weight[0]

    def unit_of(c):
        pre = saved_pre[0].reshape(experts, capacity, hidden)[:, c * part : (c + 1) * part]
        act = grad_act[0].reshape(experts, capacity, hidden)[:, c * part : (c + 1) * part]
        unit = act.astype(jnp.float32) * gelu_slope(pre.astype(jnp.float32))
        return unit.astype(jnp.bfloat16).reshape(experts * part, hidden)

    units = []
    for c in range(n_chunk):
        own = unit_of(c)
        right, left = [own], [own]
        for step in range(3):
            right.append(shift(right[-1], 1))
            left.append(shift(left[-1], -1))
        units.append(
            [own] + [jnp.where(place >= j, right[j], left[4 - j]) for j in range(1, 4)]
        )

    expert_of, position = place_slots(routes, experts, capacity)
    slot_index = expert_of * capacity + position
    token_ids = jnp.broadcast_to(
        jnp.arange(tok_dev, dtype=jnp.int32)[:, None], (tok_dev, 2)
    ).reshape(-1)
    holder = jnp.zeros((slot_count,), jnp.int32).at[slot_index.reshape(-1)].set(token_ids + 1)
    filled = holder > 0
    source_row = jnp.maximum(holder - 1, 0)
    nothing = jnp.zeros((), jnp.bfloat16)
    outgoing = jnp.where(filled[:, None], jnp.take(tokens, source_row, axis=0), nothing)
    arrived = lax.all_to_all(outgoing, "expert", split_axis=0, concat_axis=0, tiled=True)
    arrived = lax.ppermute(arrived, ("tensor", "dp"), swap_pairs(False))
    rows = lax.all_gather(arrived, "tensor", axis=0, tiled=False)
    rows = rows.reshape(4, 2, experts, n_chunk, part, width)

    returned = []
    grad_total = jnp.zeros((), jnp.float32)
    for c in range(n_chunk):
        block = jnp.concatenate(units[c], axis=0)
        partial = lax.dot_general(
            block, weight, (((1,), (1,)), ((), ())), preferred_element_type=jnp.float32
        ).astype(jnp.bfloat16)
        partial = jnp.transpose(partial.reshape(4, experts * part, 2, width), (0, 2, 1, 3))
        summed = lax.psum_scatter(
            partial.reshape(8, experts * part, width), "tensor", scatter_dimension=0, tiled=False
        )
        summed = lax.ppermute(summed, ("tensor", "dp"), swap_pairs(True))
        returned.append(
            lax.all_to_all(summed, "expert", split_axis=0, concat_axis=0, tiled=True)
        )
        rows_c = jnp.transpose(rows[:, :, :, c], (0, 2, 3, 1, 4)).reshape(-1, 2 * width)
        grad_total = grad_total + lax.dot_general(
            rows_c, block, (((0,), (0,)), ((), ())), preferred_element_type=jnp.float32
        )
    grad_block = grad_total.astype(jnp.bfloat16)
    returned = jnp.concatenate(returned, axis=0)
    where_slot = (
        (position // part) * (experts * part) + expert_of * part + position % part
    )
    first_part = jnp.take(returned, where_slot[:, 0], axis=0).astype(jnp.float32)
    second = jnp.take(returned, where_slot[:, 1], axis=0).astype(jnp.float32)
    token_grad = (first_part + second).astype(jnp.bfloat16)
    return (token_grad, grad_block[None])


def solution(mesh):
    placed = (
        P(("expert", "dp"), "tensor"),
        P(("expert", "dp"), None),
        P("expert", "dp", "tensor"),
        P("expert", "dp", "tensor"),
        P("expert", "dp", "tensor"),
    )
    return jax.shard_map(
        per_device,
        mesh=mesh,
        in_specs=placed,
        out_specs=(P(("expert", "dp"), "tensor"), P("expert", "dp", "tensor")),
        check_vma=False,
    )
```

```python
import functools

import jax
import jax.numpy as jnp
from jax import lax
from jax.experimental import pallas as pl
from jax.experimental.pallas import tpu as pltpu
from jax.sharding import PartitionSpec as P

root_coef = 0.7978845608028654
cubic_coef = 0.044715
n_chunk = 2
n_x, n_y, n_dp = 4, 4, 4
f32, bf16 = jnp.float32, jnp.bfloat16


def gelu_slope(pre_act):
    inner_arg = root_coef * (pre_act + cubic_coef * pre_act * pre_act * pre_act)
    tangent = jnp.tanh(inner_arg)
    return 0.5 * (1.0 + tangent) + 0.5 * pre_act * (1.0 - tangent * tangent) * root_coef * (
        1.0 + 3.0 * cubic_coef * pre_act * pre_act
    )


def place_slots(route_block, experts):
    tok_count = route_block.shape[0]
    ordered = jnp.transpose(route_block).reshape(-1)
    onehot = (ordered[:, None] == jnp.arange(experts, dtype=jnp.int32)[None, :]).astype(jnp.int32)
    before = jnp.cumsum(onehot, axis=0) - onehot
    position = jnp.sum(before * onehot, axis=1)
    return jnp.transpose(position.reshape(2, tok_count))


def linear(y, core, x, zh, b):
    return ((y * 2 + core) * (n_x * 2) + x * 2 + zh) * n_dp + b


def swap_pairs(flip, back):
    pairs = []
    for b in range(n_dp):
        for d in range(n_dp):
            for core in range(2):
                for x in range(n_x):
                    for zh in range(2):
                        at_batch = linear(d, core, x, zh, b)
                        at_part = linear((d - b) % n_dp, core, x, zh ^ flip, d)
                        pairs.append((at_part, at_batch) if back else (at_batch, at_part))
    return pairs


def swap(block, flip, back):
    return lax.ppermute(block, ("tensor", "expert", "dp"), swap_pairs(flip, back))


def shift_x(block, step):
    return lax.ppermute(
        block,
        "expert",
        [(x * 2 + zh, (x + step) % n_x * 2 + zh) for x in range(n_x) for zh in range(2)],
    )


def shift_y(block, step):
    return lax.ppermute(
        block,
        "tensor",
        [(y * 2 + core, (y + step) % n_y * 2 + core) for y in range(n_y) for core in range(2)],
    )


def other_core(block):
    return lax.ppermute(block, "tensor", [(t, t ^ 1) for t in range(2 * n_y)])


def shift(block, step):
    return lax.ppermute(block, "dp", [(i, i + step) for i in range(n_dp) if 0 <= i + step < n_dp])


def unit_kernel(where_ref, pre_ref, act_ref, out_ref):
    unit = act_ref[...].astype(f32) * gelu_slope(pre_ref[...].astype(f32))
    out_ref[...] = unit.astype(bf16)


def unit_of(pre, act, where, c, part):
    hidden = pre.shape[-1]
    block = (1, 1, part, hidden)
    taken = pl.BlockSpec(
        block, lambda kz, kx, w: (lax.rem(w[0] - kx + n_x, n_x), lax.rem(w[1] + kz, 2), c, 0)
    )
    size = 2 * n_x * part * hidden
    return pl.pallas_call(
        unit_kernel,
        grid_spec=pltpu.PrefetchScalarGridSpec(
            num_scalar_prefetch=1,
            grid=(2, n_x),
            in_specs=[taken, taken],
            out_specs=pl.BlockSpec(block, lambda kz, kx, w: (kz, kx, 0, 0)),
        ),
        out_shape=jax.ShapeDtypeStruct((2, n_x, part, hidden), bf16),
        cost_estimate=pl.CostEstimate(flops=16 * size, bytes_accessed=6 * size, transcendentals=size),
        compiler_params=pltpu.CompilerParams(vmem_limit_bytes=32 << 20),
    )(where, pre, act).reshape(2 * n_x * part, hidden)


def slot_kernel(rows, half, where_ref, *refs):
    own, right, left, weight = refs[0], refs[1:4], refs[4:7], refs[7]
    keep_ref, send_ref, unit, held, sems = refs[8:]
    place, y, core = where_ref[0], where_ref[1], where_ref[2]
    load_w = pltpu.make_async_copy(weight, held, sems.at[4])
    load_w.start()
    pltpu.make_async_copy(own, unit.at[0], sems.at[0]).start()
    for j in range(1, 4):

        @pl.when(place >= j)
        def _():
            pltpu.make_async_copy(right[j - 1], unit.at[j], sems.at[j]).start()

        @pl.when(place < j)
        def _():
            pltpu.make_async_copy(left[3 - j], unit.at[j], sems.at[j]).start()

    load_w.wait()
    kept = pl.multiple_of(core * half, half)
    sent = pl.multiple_of((1 - core) * half, half)
    for j in range(4):
        pltpu.make_async_copy(own, unit.at[j], sems.at[j]).wait()
        slot = lax.rem(j - y + n_y, n_y)
        for start, out in ((kept, keep_ref), (sent, send_ref)):
            out[slot] = lax.dot_general(
                unit[j],
                held[pl.ds(start, half), :],
                (((1,), (1,)), ((), ())),
                preferred_element_type=f32,
            ).astype(bf16)


def slot_part(own, right, left, weight, where):
    rows, hidden = own.shape
    width = weight.shape[0]
    half = width // 2
    anywhere = pl.BlockSpec(memory_space=pl.ANY)
    whole = pl.BlockSpec(memory_space=pltpu.VMEM)
    return pl.pallas_call(
        functools.partial(slot_kernel, rows, half),
        in_specs=[pl.BlockSpec(memory_space=pltpu.SMEM)] + [anywhere] * 8,
        out_specs=[whole, whole],
        out_shape=[jax.ShapeDtypeStruct((4, rows, half), bf16)] * 2,
        scratch_shapes=[
            pltpu.VMEM((4, rows, hidden), bf16),
            pltpu.VMEM((width, hidden), bf16),
            pltpu.SemaphoreType.DMA((5,)),
        ],
        cost_estimate=pl.CostEstimate(
            flops=8 * rows * hidden * width,
            bytes_accessed=2 * hidden * (4 * rows + width),
            transcendentals=0,
        ),
        compiler_params=pltpu.CompilerParams(vmem_limit_bytes=40 << 20),
    )(where, own, *right, *left, weight)


def grad_kernel(rows, half, where_ref, x_ref, *refs):
    out_ref = refs[-1]
    place = where_ref[0]
    totals = [None, None]
    for c in range(n_chunk):
        group = refs[7 * c : 7 * c + 7]
        for j in range(4):
            if j == 0:
                unit = group[0][...]
            else:
                unit = jnp.where(place >= j, group[j][...], group[7 - j][...])
            for h in range(2):
                term = jnp.dot(
                    x_ref[2 * j + h, :, c * rows : (c + 1) * rows], unit, preferred_element_type=f32
                )
                totals[h] = term if totals[h] is None else totals[h] + term
    for h in range(2):
        out_ref[h * half : (h + 1) * half, :] = totals[h].astype(bf16)


def grad_of(columns, units, where):
    half, all_rows = columns.shape[1:]
    rows = all_rows // n_chunk
    hidden = units[0].shape[1]
    tile = 256
    return pl.pallas_call(
        functools.partial(grad_kernel, rows, half),
        grid=(hidden // tile,),
        in_specs=[
            pl.BlockSpec(memory_space=pltpu.SMEM),
            pl.BlockSpec(columns.shape, lambda i: (0, 0, 0)),
        ]
        + [pl.BlockSpec((rows, tile), lambda i: (0, i))] * len(units),
        out_specs=pl.BlockSpec((2 * half, tile), lambda i: (0, i)),
        out_shape=jax.ShapeDtypeStruct((2 * half, hidden), bf16),
        cost_estimate=pl.CostEstimate(
            flops=16 * half * all_rows * hidden,
            bytes_accessed=2 * (columns.size + len(units) * rows * hidden + 2 * half * hidden),
            transcendentals=0,
        ),
        compiler_params=pltpu.CompilerParams(vmem_limit_bytes=40 << 20),
    )(where, columns, *units)


def per_device(tokens, routes, up_weight, saved_pre, grad_act):
    experts = lax.axis_size("expert")
    place = lax.axis_index("dp")
    tensor, expert = lax.axis_index("tensor"), lax.axis_index("expert")
    my_x, my_zh = expert // 2, expert % 2
    slot_count, hidden = saved_pre.shape[1:]
    capacity = slot_count // experts
    part = capacity // n_chunk
    tok_dev, width = tokens.shape
    weight = up_weight[0]
    pre = saved_pre.reshape(n_x, 2, capacity, hidden)
    act = grad_act.reshape(n_x, 2, capacity, hidden)
    group_at = jnp.stack([my_x, my_zh]).astype(jnp.int32)
    device_at = jnp.stack([place, tensor // 2, tensor % 2]).astype(jnp.int32)

    owns = [unit_of(pre, act, group_at, c, part) for c in range(n_chunk)]
    right, left = [[o] for o in owns], [[o] for o in owns]

    def step(c):
        right[c].append(shift(right[c][-1], 1))
        left[c].append(shift(left[c][-1], -1))

    for c in range(n_chunk):
        step(c)

    position = place_slots(routes, experts)
    kx = (routes // 2 - my_x) % n_x
    kz = (routes + my_zh) % 2
    row_of = (kz * n_x + kx) * capacity + position
    numbers = jnp.arange(slot_count, dtype=jnp.int32)
    holds = (row_of[:, 0, None] == numbers) | (row_of[:, 1, None] == numbers)
    outgoing = lax.dot_general(
        holds.astype(bf16), tokens, (((0,), (0,)), ((), ())), preferred_element_type=f32
    ).astype(bf16).reshape(2, n_x, capacity, width)
    outgoing, owns[0] = lax.optimization_barrier((outgoing, owns[0]))
    at_x = [outgoing[:, 0]] + [shift_x(outgoing[:, k], k) for k in range(1, n_x)]
    at_x = jnp.stack(at_x, axis=1)
    arrived = jnp.stack([swap(at_x[k], k, False) for k in range(2)])
    arrived = arrived.reshape(2 * n_x, n_chunk, part, width)
    arrived = jnp.transpose(arrived, (3, 1, 0, 2)).reshape(width, slot_count)
    columns = lax.all_gather(arrived, "tensor", axis=0, tiled=False)

    (right[0][1], left[0][1]), arrived = lax.optimization_barrier(
        ((right[0][1], left[0][1]), arrived)
    )
    step(0)
    step(1)
    step(0)
    step(1)

    returned = []
    for c in range(n_chunk):
        keep, send = slot_part(owns[c], right[c][1:], left[c][1:], weight, device_at)
        got = other_core(send)
        both = keep.astype(f32) + got.astype(f32)
        gathered = [shift_y(both[k].astype(bf16), k) for k in range(1, n_y)]
        summed = both[0]
        for block in gathered:
            summed = summed + block.astype(f32)
        summed = summed.astype(bf16).reshape(2, n_x * part, width)
        home = jnp.stack([swap(summed[k], k, True) for k in range(2)])
        home = home.reshape(2, n_x, part, width)
        at_home = [home[:, 0]] + [shift_x(home[:, k], -k) for k in range(1, n_x)]
        returned.append(jnp.stack(at_home, axis=1).reshape(2 * n_x * part, width))

    units = []
    for c in range(n_chunk):
        units += [owns[c]] + right[c][1:] + left[c][1:]
    grad_block = grad_of(columns, units, device_at)

    token_grad = jnp.zeros((tok_dev, width), f32)
    part_numbers = jnp.arange(2 * n_x * part, dtype=jnp.int32)
    row_in_part = (kz * n_x + kx) * part + position % part
    for c in range(n_chunk):
        row_c = jnp.where(position // part == c, row_in_part, -1)
        holds_c = (row_c[:, 0, None] == part_numbers) | (row_c[:, 1, None] == part_numbers)
        token_grad = token_grad + jnp.dot(
            holds_c.astype(bf16), returned[c], preferred_element_type=f32
        )
    return (token_grad.astype(bf16), grad_block[None])


def solution(mesh):
    placed = (
        P(("expert", "dp"), "tensor"),
        P(("expert", "dp"), None),
        P("expert", "dp", "tensor"),
        P("expert", "dp", "tensor"),
        P("expert", "dp", "tensor"),
    )
    return jax.shard_map(
        per_device,
        mesh=mesh,
        in_specs=placed,
        out_specs=(P(("expert", "dp"), "tensor"), P("expert", "dp", "tensor")),
        check_vma=False,
    )
```

```python
import functools

import jax
import jax.numpy as jnp
from jax import lax
from jax.experimental import pallas as pl
from jax.experimental.pallas import tpu as pltpu
from jax.sharding import PartitionSpec as P

root_coef = 0.7978845608028654
cubic_coef = 0.044715
n_chunk = 2
n_x, n_y, n_dp = 4, 4, 4
f32, bf16 = jnp.float32, jnp.bfloat16


def gelu_slope(pre_act):
    inner_arg = root_coef * (pre_act + cubic_coef * pre_act * pre_act * pre_act)
    tangent = jnp.tanh(inner_arg)
    return 0.5 * (1.0 + tangent) + 0.5 * pre_act * (1.0 - tangent * tangent) * root_coef * (
        1.0 + 3.0 * cubic_coef * pre_act * pre_act
    )


def place_slots(route_block, experts):
    tok_count = route_block.shape[0]
    ordered = jnp.transpose(route_block).reshape(-1)
    onehot = (ordered[:, None] == jnp.arange(experts, dtype=jnp.int32)[None, :]).astype(jnp.int32)
    before = jnp.cumsum(onehot, axis=0) - onehot
    position = jnp.sum(before * onehot, axis=1)
    return jnp.transpose(position.reshape(2, tok_count))


def linear(y, core, x, zh, b):
    return ((y * 2 + core) * (n_x * 2) + x * 2 + zh) * n_dp + b


def swap_pairs(flip, back):
    pairs = []
    for b in range(n_dp):
        for d in range(n_dp):
            for core in range(2):
                for x in range(n_x):
                    for zh in range(2):
                        at_batch = linear(d, core, x, zh, b)
                        at_part = linear((d - b) % n_dp, core, x, zh ^ flip, d)
                        pairs.append((at_part, at_batch) if back else (at_batch, at_part))
    return pairs


def swap(block, flip, back):
    return lax.ppermute(block, ("tensor", "expert", "dp"), swap_pairs(flip, back))


def shift_x(block, step):
    return lax.ppermute(
        block,
        "expert",
        [(x * 2 + zh, (x + step) % n_x * 2 + zh) for x in range(n_x) for zh in range(2)],
    )


def shift_y(block, step):
    return lax.ppermute(
        block,
        "tensor",
        [(y * 2 + core, (y + step) % n_y * 2 + core) for y in range(n_y) for core in range(2)],
    )


def other_core(block):
    return lax.ppermute(block, "tensor", [(t, t ^ 1) for t in range(2 * n_y)])


def shift(block, step):
    return lax.ppermute(block, "dp", [(i, i + step) for i in range(n_dp) if 0 <= i + step < n_dp])


def unit_kernel(where_ref, pre_ref, act_ref, out_ref):
    unit = act_ref[...].astype(f32) * gelu_slope(pre_ref[...].astype(f32))
    out_ref[...] = unit.astype(bf16)


def unit_of(pre, act, where, c, part):
    hidden = pre.shape[-1]
    block = (1, 1, part, hidden)
    taken = pl.BlockSpec(
        block, lambda kz, kx, w: (lax.rem(w[0] - kx + n_x, n_x), lax.rem(w[1] + kz, 2), c, 0)
    )
    size = 2 * n_x * part * hidden
    return pl.pallas_call(
        unit_kernel,
        grid_spec=pltpu.PrefetchScalarGridSpec(
            num_scalar_prefetch=1,
            grid=(2, n_x),
            in_specs=[taken, taken],
            out_specs=pl.BlockSpec(block, lambda kz, kx, w: (kz, kx, 0, 0)),
        ),
        out_shape=jax.ShapeDtypeStruct((2, n_x, part, hidden), bf16),
        cost_estimate=pl.CostEstimate(flops=16 * size, bytes_accessed=6 * size, transcendentals=size),
        compiler_params=pltpu.CompilerParams(vmem_limit_bytes=32 << 20),
    )(where, pre, act).reshape(2 * n_x * part, hidden)


def slot_kernel(rows, half, where_ref, *refs):
    own, right, left, weight = refs[0], refs[1:4], refs[4:7], refs[7]
    keep_ref, send_ref, unit, held, sems = refs[8:]
    place, y, core = where_ref[0], where_ref[1], where_ref[2]
    load_w = pltpu.make_async_copy(weight, held, sems.at[4])
    load_w.start()
    pltpu.make_async_copy(own, unit.at[0], sems.at[0]).start()
    for j in range(1, 4):

        @pl.when(place >= j)
        def _():
            pltpu.make_async_copy(right[j - 1], unit.at[j], sems.at[j]).start()

        @pl.when(place < j)
        def _():
            pltpu.make_async_copy(left[3 - j], unit.at[j], sems.at[j]).start()

    load_w.wait()
    kept = pl.multiple_of(core * half, half)
    sent = pl.multiple_of((1 - core) * half, half)
    for j in range(4):
        pltpu.make_async_copy(own, unit.at[j], sems.at[j]).wait()
        slot = lax.rem(j - y + n_y, n_y)
        for start, out in ((kept, keep_ref), (sent, send_ref)):
            out[slot] = lax.dot_general(
                unit[j],
                held[pl.ds(start, half), :],
                (((1,), (1,)), ((), ())),
                preferred_element_type=f32,
            ).astype(bf16)


def slot_part(own, right, left, weight, where):
    rows, hidden = own.shape
    width = weight.shape[0]
    half = width // 2
    anywhere = pl.BlockSpec(memory_space=pl.ANY)
    whole = pl.BlockSpec(memory_space=pltpu.VMEM)
    return pl.pallas_call(
        functools.partial(slot_kernel, rows, half),
        in_specs=[pl.BlockSpec(memory_space=pltpu.SMEM)] + [anywhere] * 8,
        out_specs=[whole, whole],
        out_shape=[jax.ShapeDtypeStruct((4, rows, half), bf16)] * 2,
        scratch_shapes=[
            pltpu.VMEM((4, rows, hidden), bf16),
            pltpu.VMEM((width, hidden), bf16),
            pltpu.SemaphoreType.DMA((5,)),
        ],
        cost_estimate=pl.CostEstimate(
            flops=8 * rows * hidden * width,
            bytes_accessed=2 * hidden * (4 * rows + width),
            transcendentals=0,
        ),
        compiler_params=pltpu.CompilerParams(vmem_limit_bytes=40 << 20),
    )(where, own, *right, *left, weight)


def grad_kernel(rows, half, where_ref, x_ref, *refs):
    out_ref = refs[-1]
    place = where_ref[0]
    totals = [None, None]
    for c in range(n_chunk):
        group = refs[7 * c : 7 * c + 7]
        for j in range(4):
            if j == 0:
                unit = group[0][...]
            else:
                unit = jnp.where(place >= j, group[j][...], group[7 - j][...])
            for h in range(2):
                term = jnp.dot(
                    x_ref[2 * j + h, :, c * rows : (c + 1) * rows], unit, preferred_element_type=f32
                )
                totals[h] = term if totals[h] is None else totals[h] + term
    for h in range(2):
        out_ref[h * half : (h + 1) * half, :] = totals[h].astype(bf16)


def grad_of(columns, units, where):
    half, all_rows = columns.shape[1:]
    rows = all_rows // n_chunk
    hidden = units[0].shape[1]
    tile = 512
    return pl.pallas_call(
        functools.partial(grad_kernel, rows, half),
        grid=(hidden // tile,),
        in_specs=[
            pl.BlockSpec(memory_space=pltpu.SMEM),
            pl.BlockSpec(columns.shape, lambda i: (0, 0, 0)),
        ]
        + [pl.BlockSpec((rows, tile), lambda i: (0, i))] * len(units),
        out_specs=pl.BlockSpec((2 * half, tile), lambda i: (0, i)),
        out_shape=jax.ShapeDtypeStruct((2 * half, hidden), bf16),
        cost_estimate=pl.CostEstimate(
            flops=16 * half * all_rows * hidden,
            bytes_accessed=2 * (columns.size + len(units) * rows * hidden + 2 * half * hidden),
            transcendentals=0,
        ),
        compiler_params=pltpu.CompilerParams(vmem_limit_bytes=48 << 20),
    )(where, columns, *units)


def per_device(tokens, routes, up_weight, saved_pre, grad_act):
    experts = lax.axis_size("expert")
    place = lax.axis_index("dp")
    tensor, expert = lax.axis_index("tensor"), lax.axis_index("expert")
    my_x, my_zh = expert // 2, expert % 2
    slot_count, hidden = saved_pre.shape[1:]
    capacity = slot_count // experts
    part = capacity // n_chunk
    tok_dev, width = tokens.shape
    weight = up_weight[0]
    pre = saved_pre.reshape(n_x, 2, capacity, hidden)
    act = grad_act.reshape(n_x, 2, capacity, hidden)
    group_at = jnp.stack([my_x, my_zh]).astype(jnp.int32)
    device_at = jnp.stack([place, tensor // 2, tensor % 2]).astype(jnp.int32)

    owns = [unit_of(pre, act, group_at, c, part) for c in range(n_chunk)]
    right, left = [[o] for o in owns], [[o] for o in owns]

    def step(c):
        right[c].append(shift(right[c][-1], 1))
        left[c].append(shift(left[c][-1], -1))

    for c in range(n_chunk):
        step(c)

    position = place_slots(routes, experts)
    kx = (routes // 2 - my_x) % n_x
    kz = (routes + my_zh) % 2
    row_of = (kz * n_x + kx) * capacity + position
    numbers = jnp.arange(slot_count, dtype=jnp.int32)
    holds = (row_of[:, 0, None] == numbers) | (row_of[:, 1, None] == numbers)
    outgoing = lax.dot_general(
        holds.astype(bf16), tokens, (((0,), (0,)), ((), ())), preferred_element_type=f32
    ).astype(bf16).reshape(2, n_x, capacity, width)
    outgoing, owns[0] = lax.optimization_barrier((outgoing, owns[0]))
    at_x = [outgoing[:, 0]] + [shift_x(outgoing[:, k], k) for k in range(1, n_x)]
    at_x = jnp.stack(at_x, axis=1)
    arrived = jnp.stack([swap(at_x[k], k, False) for k in range(2)])
    arrived = arrived.reshape(2 * n_x, n_chunk, part, width)
    arrived = jnp.transpose(arrived, (3, 1, 0, 2)).reshape(width, slot_count)
    columns = lax.all_gather(arrived, "tensor", axis=0, tiled=False)

    (right[0][1], left[0][1]), arrived = lax.optimization_barrier(
        ((right[0][1], left[0][1]), arrived)
    )
    step(0)
    step(1)
    step(0)
    step(1)

    returned = []
    for c in range(n_chunk):
        keep, send = slot_part(owns[c], right[c][1:], left[c][1:], weight, device_at)
        got = other_core(send)
        both = keep.astype(f32) + got.astype(f32)
        gathered = [shift_y(both[k].astype(bf16), k) for k in range(1, n_y)]
        summed = both[0]
        for block in gathered:
            summed = summed + block.astype(f32)
        summed = summed.astype(bf16).reshape(2, n_x * part, width)
        home = jnp.stack([swap(summed[k], k, True) for k in range(2)])
        home = home.reshape(2, n_x, part, width)
        at_home = [home[:, 0]] + [shift_x(home[:, k], -k) for k in range(1, n_x)]
        returned.append(jnp.stack(at_home, axis=1).reshape(2 * n_x * part, width))

    units = []
    for c in range(n_chunk):
        units += [owns[c]] + right[c][1:] + left[c][1:]
    grad_block = grad_of(columns, units, device_at)

    token_grad = jnp.zeros((tok_dev, width), f32)
    part_numbers = jnp.arange(2 * n_x * part, dtype=jnp.int32)
    row_in_part = (kz * n_x + kx) * part + position % part
    for c in range(n_chunk):
        row_c = jnp.where(position // part == c, row_in_part, -1)
        holds_c = (row_c[:, 0, None] == part_numbers) | (row_c[:, 1, None] == part_numbers)
        token_grad = token_grad + jnp.dot(
            holds_c.astype(bf16), returned[c], preferred_element_type=f32
        )
    return (token_grad.astype(bf16), grad_block[None])


def solution(mesh):
    placed = (
        P(("expert", "dp"), "tensor"),
        P(("expert", "dp"), None),
        P("expert", "dp", "tensor"),
        P("expert", "dp", "tensor"),
        P("expert", "dp", "tensor"),
    )
    return jax.shard_map(
        per_device,
        mesh=mesh,
        in_specs=placed,
        out_specs=(P(("expert", "dp"), "tensor"), P("expert", "dp", "tensor")),
        check_vma=False,
    )
```
